32 devices in a mesh: section: 2 (over core), dp: 8 (over z, y), cls: 2 (over x).
Axes of the slice: x: 2, y: 2, z: 4, core: 2. Of those that a mesh axis runs over, the one named last changes fastest.
Arguments:
- embeddings: bfloat16 [1024, 512], P('dp')
- centers: bfloat16 [131072, 512], P(('section', 'dp', 'cls'))
- sample_ids: int32 [32, 1536], P(('section', 'dp', 'cls')), may hold values from 0 to 4095, as said below
- labels: int32 [1024], P('dp'), may hold values from 0 to 131071, as said below
Outputs:
- feature_grad: float32 [1024, 512], P(('section', 'dp', 'cls'))
- row_loss: float32 [1024], P('dp')
The draws below stay inside these ranges and needn't reach their ends.
Inputs may be any that keep to these rules, and one draw needn't show every extreme that they name: `sample_ids`: the 1536 entries of each row are distinct. For each row, labels // 4096 names a shard j, and labels % 4096 is among sample_ids[j].
All inputs are finite; a program needn't handle non-finite values.
Results may differ from the reference program's by a relative error of at most 0.0033.
Values may be sent and summed in bfloat16 or wider, within the bound.
A program may use at most 64 MiB of HBM per device.

```python
import jax
import jax.numpy as jnp
from jax import lax

D = 512
CLS_DEV = 4096
K = 1536
SHARDS = 32
CLASSES = 131072
ROWS = 1024


def shard_orders(key):
    keys = jax.random.split(jax.random.fold_in(key, 7), SHARDS)
    return jax.vmap(lambda one_key: jax.random.permutation(one_key, CLS_DEV))(keys).astype(jnp.int32)


def draw_sample_ids(key, part):
    orders = shard_orders(key)
    return orders[:, :K].astype(jnp.int32)


def draw_labels(key, part):
    orders = shard_orders(key)
    shard_pick = jax.random.randint(jax.random.fold_in(key, 11), (ROWS,), 0, SHARDS)
    slot_pick = jax.random.randint(jax.random.fold_in(key, 13), (ROWS,), 0, K // 2)
    inside = orders[shard_pick, slot_pick]
    return (shard_pick * CLS_DEV + inside).astype(jnp.int32)


def draw_embeddings(key, part):
    first_key = jax.random.fold_in(key, 21)
    second_key = jax.random.fold_in(key, 22)
    base = jax.random.normal(first_key, (ROWS, D), jnp.float32)
    scales = jnp.exp(jax.random.uniform(second_key, (ROWS, 1), jnp.float32, jnp.log(0.3), jnp.log(3.0)))
    return (base * scales / jnp.sqrt(jnp.float32(D))).astype(jnp.bfloat16)


def draw_centers(key, part):
    first_key = jax.random.fold_in(key, 31)
    second_key = jax.random.fold_in(key, 32)
    base = jax.random.normal(first_key, (CLASSES, D), jnp.float32)
    scales = jnp.exp(jax.random.uniform(second_key, (CLASSES, 1), jnp.float32, 0.0, jnp.log(10.0)))
    return (base * scales / jnp.sqrt(jnp.float32(D))).astype(jnp.bfloat16)


def setup_inputs(seed: int = 0) -> dict:
    key_of = jax.random.split(jax.random.key(seed), 5)
    embeddings = draw_embeddings(jax.random.fold_in(key_of[4], 71), 0)
    centers = draw_centers(jax.random.fold_in(key_of[4], 71), 0)
    sample_ids = draw_sample_ids(jax.random.fold_in(key_of[4], 71), 0)
    labels = draw_labels(jax.random.fold_in(key_of[4], 71), 0)
    return dict(embeddings=embeddings, centers=centers, sample_ids=sample_ids, labels=labels)


LOGIT_SCALE = 64.0
MARGIN = 0.35
EPSILON = 1e-06

def reference(embeddings, centers, sample_ids, labels):
    shard_count = sample_ids.shape[0]
    width = embeddings.shape[1]
    row_count = embeddings.shape[0]
    emb_float = embeddings.astype(jnp.float32)
    row_norm = jnp.sqrt(lax.optimization_barrier(jnp.sum(emb_float * emb_float, axis=1)) + EPSILON)
    unit_rows = (emb_float / row_norm[:, None]).astype(jnp.bfloat16)
    center_blocks = centers.reshape(shard_count, CLS_DEV, width)
    shard_numbers = jnp.arange(shard_count, dtype=jnp.int32)

    def one_shard(carry, inputs):
        total, target, unscaled, own = carry
        block, ids, number = inputs
        global_ids = (ids + number * CLS_DEV).astype(jnp.int32)
        chosen = jnp.take(block, ids, axis=0).astype(jnp.float32)
        center_norm = jnp.sqrt(lax.optimization_barrier(jnp.sum(chosen * chosen, axis=1)) + EPSILON)
        unit_centers = (chosen / center_norm[:, None]).astype(jnp.bfloat16)
        cosine = jnp.dot(unit_rows, unit_centers.T, preferred_element_type=jnp.float32)
        matches = global_ids[None, :] == labels[:, None]
        logits = LOGIT_SCALE * cosine - LOGIT_SCALE * MARGIN * matches.astype(cosine.dtype)
        exponent = jnp.exp(logits)
        total = total + lax.optimization_barrier(jnp.sum(exponent, axis=1))
        target = target + lax.optimization_barrier(jnp.sum(jnp.where(matches, logits, jnp.zeros_like(logits)), axis=1))
        weights = exponent.astype(jnp.bfloat16)
        unscaled = unscaled + jnp.dot(weights, unit_centers, preferred_element_type=jnp.float32)
        own = own + jnp.dot(matches.astype(jnp.bfloat16), unit_centers, preferred_element_type=jnp.float32)
        return ((total, target, unscaled, own), None)
    start = (jnp.zeros((row_count,), jnp.float32), jnp.zeros((row_count,), jnp.float32), jnp.zeros((row_count, width), jnp.float32), jnp.zeros((row_count, width), jnp.float32))
    (total, target, unscaled, own_center), _ = lax.scan(one_shard, start, (center_blocks, sample_ids, shard_numbers))
    row_loss = jnp.log(total) - target
    unit_grad = LOGIT_SCALE * (unscaled / total[:, None] - own_center)
    unit_float = emb_float / row_norm[:, None]
    along = lax.optimization_barrier(jnp.sum(unit_float * unit_grad, axis=1, keepdims=True))
    feature_grad = (unit_grad - unit_float * along) / row_norm[:, None]
    return (feature_grad, row_loss)
```

```python
import functools

import jax
import jax.numpy as jnp
from jax import lax
from jax.experimental import pallas as pl
from jax.experimental.pallas import tpu as pltpu
from jax.sharding import PartitionSpec as P

LOGIT_SCALE = 64.0
MARGIN = 0.35
EPSILON = 1e-06
LANES = 128
PICK_STEPS = 8
CHUNKS = 4
MESH = pl.DeviceIdType.MESH


def to_column(row):
    return jnp.transpose(jnp.broadcast_to(row, (LANES, LANES)))


def to_row(column):
    return jnp.transpose(jnp.broadcast_to(column, (LANES, LANES)))[:1, :]


def kernel(
    n_dp, n_cls,
    emb_ref, centers_hbm, ids_ref, labels_ref,
    grad_ref, loss_ref,
    centers, gathered, labels, ids_column, unit_centers, weights, onehot,
    sums, group_sums, all_sums,
    unscaled, own, unscaled_in, own_in, inverse,
    cls_out, cls_in, kept, dp_out, dp_in,
    centers_sem,
    dp_send, dp_recv, label_send, label_recv, cls_send, cls_recv, sec_send, sec_recv,
    group_send, group_recv, all_send, all_recv, half_send, half_recv,
    rows_send, rows_recv, piece_send, piece_recv,
):
    sec, dp, cls = lax.axis_index("section"), lax.axis_index("dp"), lax.axis_index("cls")
    n_group = 2 * n_cls
    group = sec * n_cls + cls
    shard = (sec * n_dp + dp) * n_cls + cls
    other = 1 - sec
    n_pieces, rh, width = emb_ref.shape
    per_shard = centers_hbm.shape[0]
    k_total = ids_ref.shape[1]
    half_pieces = n_dp * n_cls
    pieces_per_unit = 2 * n_pieces
    rows_per_unit = 2 * LANES

    def dp_peer(k):
        return lax.rem(dp + k, n_dp)

    def dp_source(k):
        return lax.rem(dp + n_dp - k, n_dp)

    def cls_peer(j):
        return lax.rem(cls + j, n_cls)

    def group_peer(j):
        g = lax.rem(group + j, n_group)
        return (g // n_cls, dp, lax.rem(g, n_cls))

    def remote(src, dst, send, recv, device):
        return pltpu.make_async_remote_copy(
            src_ref=src, dst_ref=dst, send_sem=send, recv_sem=recv,
            device_id=device, device_id_type=MESH,
        )

    load = pltpu.make_async_copy(centers_hbm, centers, centers_sem)
    load.start()

    barrier = pltpu.get_barrier_semaphore()
    for k in range(1, n_dp):
        pl.semaphore_signal(barrier, inc=1, device_id=(sec, dp_peer(k), cls), device_id_type=MESH)
    for j in range(1, n_group):
        pl.semaphore_signal(barrier, inc=1, device_id=group_peer(j), device_id_type=MESH)

    gathered[dp] = emb_ref[...]
    labels[dp] = labels_ref[...]
    ids_float = ids_ref[...].astype(jnp.float32)
    for i in range(k_total // LANES):
        ids_column[i * LANES:(i + 1) * LANES, :] = to_column(ids_float[:, i * LANES:(i + 1) * LANES])

    pl.semaphore_wait(barrier, n_dp - 1 + n_group - 1)

    def block_copy(k):
        return remote(
            emb_ref.at[group], gathered.at[dp, group], dp_send.at[k], dp_recv.at[k], (sec, dp_peer(k), cls)
        )

    def block_arrival(k):
        there = gathered.at[dp_source(k), group]
        return remote(there, there, dp_send.at[k], dp_recv.at[k], (sec, dp_peer(k), cls))

    def label_copy(k):
        return remote(labels_ref, labels.at[dp], label_send.at[k], label_recv.at[k], (sec, dp_peer(k), cls))

    def label_arrival(k):
        there = labels.at[dp_source(k)]
        return remote(there, there, label_send.at[k], label_recv.at[k], (sec, dp_peer(k), cls))

    def cls_copy(k, j):
        piece = gathered.at[dp_source(k), group]
        return remote(piece, piece, cls_send.at[j, k], cls_recv.at[j, k], (sec, dp, cls_peer(j)))

    def cls_arrival(k, j):
        piece = gathered.at[dp_source(k), sec * n_cls + lax.rem(cls + n_cls - j, n_cls)]
        return remote(piece, piece, cls_send.at[j, k], cls_recv.at[j, k], (sec, dp, cls_peer(j)))

    def sec_copy(k, owner):
        pieces = gathered.at[dp_source(k), pl.ds(owner * n_cls, n_cls)]
        return remote(pieces, pieces, sec_send.at[k], sec_recv.at[k], (other, dp, cls))

    for k in range(1, n_dp):
        block_copy(k).start()
    for k in range(1, n_dp):
        label_copy(k).start()

    def pass_to_cls(k):
        block_arrival(k).wait_recv()
        for j in range(1, n_cls):
            cls_copy(k, j).start()

    def pass_to_sec(k):
        for j in range(1, n_cls):
            cls_arrival(k, j).wait_recv()
        sec_copy(k, sec).start()

    load.wait()
    step_rows = k_total // PICK_STEPS
    per_step = n_dp // PICK_STEPS
    lag = 2 * per_step

    def pick(t, carry):
        for i in range(per_step):
            k = t * per_step + i

            @pl.when(k >= 1)
            def _():
                pass_to_cls(k)

            @pl.when(k - lag >= 1)
            def _():
                pass_to_sec(k - lag)

        start = pl.multiple_of(t * step_rows, step_rows)
        wanted = ids_column[pl.ds(start, step_rows), :]
        lane = lax.broadcasted_iota(jnp.int32, (step_rows, LANES), 1).astype(jnp.float32)
        pieces = []
        for i in range(per_shard // LANES):
            hit = wanted == lane + jnp.float32(i * LANES)
            pieces.append(jnp.where(hit, jnp.float32(1.0), jnp.float32(0.0)).astype(jnp.bfloat16))
        chosen = jnp.dot(jnp.concatenate(pieces, axis=1), centers[...], preferred_element_type=jnp.float32)
        norm = jnp.sqrt(jnp.sum(chosen * chosen, axis=1, keepdims=True) + EPSILON)
        unit_centers[pl.ds(start, step_rows), :] = (chosen * (1.0 / norm)).astype(jnp.bfloat16)
        return carry

    lax.fori_loop(0, PICK_STEPS, pick, 0)
    for k in range(n_dp - lag, n_dp):
        pass_to_sec(k)
    for k in range(1, n_dp):
        label_arrival(k).wait_recv()
    for k in range(1, n_dp):
        sec_copy(k, other).wait_recv()

    def score(u, carry):
        rows = gathered[pl.ds(2 * u, 2)].astype(jnp.float32).reshape(rows_per_unit, width)
        norm = jnp.sqrt(jnp.sum(rows * rows, axis=1, keepdims=True) + EPSILON)
        unit_rows = (rows * (1.0 / norm)).astype(jnp.bfloat16)
        local = []
        for i in range(2):
            local.append(to_column((labels[2 * u + i] - shard * per_shard).astype(jnp.float32)))
        local = jnp.concatenate(local, axis=0)
        cosine = lax.dot_general(
            unit_rows, unit_centers[...], (((1,), (1,)), ((), ())), preferred_element_type=jnp.float32
        )
        start = pl.multiple_of(u * rows_per_unit, rows_per_unit)
        total = jnp.zeros((rows_per_unit, LANES), jnp.float32)
        target = jnp.zeros((rows_per_unit, LANES), jnp.float32)
        for i in range(k_total // LANES):
            columns = slice(i * LANES, (i + 1) * LANES)
            matches = local == ids_ref[:, columns].astype(jnp.float32)
            logits = LOGIT_SCALE * cosine[:, columns]
            logits = jnp.where(matches, logits - LOGIT_SCALE * MARGIN, logits)
            exponent = jnp.exp(logits)
            total = total + exponent
            target = target + jnp.where(matches, logits, jnp.float32(0.0))
            weights[pl.ds(start, rows_per_unit), columns] = exponent.astype(jnp.bfloat16)
            onehot[pl.ds(start, rows_per_unit), columns] = jnp.where(
                matches, jnp.float32(1.0), jnp.float32(0.0)
            ).astype(jnp.bfloat16)
        total = jnp.sum(total, axis=1, keepdims=True)
        target = jnp.sum(target, axis=1, keepdims=True)
        for i in range(2):
            part = slice(i * LANES, (i + 1) * LANES)
            sums[2 * u + i] = jnp.concatenate([to_row(total[part]), to_row(target[part])], axis=0)
        return carry

    lax.fori_loop(0, n_dp // 2, score, 0)

    group_sums[group] = sums[...]

    def group_copy(j):
        return remote(sums, group_sums.at[group], group_send.at[j], group_recv.at[j], group_peer(j))

    def group_arrival(j):
        there = group_sums.at[lax.rem(group + n_group - j, n_group)]
        return remote(there, there, group_send.at[j], group_recv.at[j], group_peer(j))

    def all_copy(k):
        return remote(
            all_sums.at[dp], all_sums.at[dp], all_send.at[k], all_recv.at[k], (sec, dp_peer(k), cls)
        )

    def all_arrival(k):
        there = all_sums.at[dp_source(k)]
        return remote(there, there, all_send.at[k], all_recv.at[k], (sec, dp_peer(k), cls))

    for j in range(1, n_group):
        group_copy(j).start()

    units_per_half = n_dp // 4

    def weigh_half(half):
        def weigh(i, carry):
            u = half * units_per_half + i
            start = pl.multiple_of(u * rows_per_unit, rows_per_unit)
            dst = pl.ds(i * pieces_per_unit, pieces_per_unit)
            shape = (pieces_per_unit, rh, width)
            unscaled[half, dst] = jnp.dot(
                weights[pl.ds(start, rows_per_unit), :], unit_centers[...], preferred_element_type=jnp.float32
            ).reshape(shape)
            own[half, dst] = jnp.dot(
                onehot[pl.ds(start, rows_per_unit), :], unit_centers[...], preferred_element_type=jnp.float32
            ).reshape(shape).astype(jnp.bfloat16)
            return carry

        lax.fori_loop(0, units_per_half, weigh, 0)

    weigh_half(other)
    half_copies = [
        remote(unscaled.at[other], unscaled_in, half_send.at[0], half_recv.at[0], (other, dp, cls)),
        remote(own.at[other], own_in, half_send.at[1], half_recv.at[1], (other, dp, cls)),
    ]
    for copy in half_copies:
        copy.start()

    for j in range(1, n_group):
        group_arrival(j).wait_recv()
    group_total = group_sums[0]
    for j in range(1, n_group):
        group_total = group_total + group_sums[j]
    all_sums[dp] = group_total
    for k in range(1, n_dp):
        all_copy(k).start()

    weigh_half(sec)

    for k in range(1, n_dp):
        all_arrival(k).wait_recv()
    sums_all = all_sums[0]
    for k in range(1, n_dp):
        sums_all = sums_all + all_sums[k]
    group_sums[group] = sums_all
    mine = group_sums[group, dp]
    loss_ref[...] = jnp.log(mine[:1, :]) - mine[1:, :]
    for b in range(n_dp // 2):
        block = group_sums[group, sec * (n_dp // 2) + b]
        inverse[b * n_pieces:(b + 1) * n_pieces] = to_column(LOGIT_SCALE / block[:1, :]).reshape(
            n_pieces, rh, LANES
        )
    for copy in half_copies:
        copy.wait_recv()

    def gradient(k, column):
        p = dp_peer(k) * n_cls + column
        scale = jnp.concatenate([inverse[p]] * (width // LANES), axis=1)
        centers_here = own[sec, p].astype(jnp.float32) + own_in[p].astype(jnp.float32)
        return (unscaled[sec, p] + unscaled_in[p]) * scale - LOGIT_SCALE * centers_here

    per_chunk = n_dp // CHUNKS

    def rows_copy(j, q):
        part = pl.ds(q * per_chunk, per_chunk)
        return remote(
            cls_out.at[j, part], cls_in.at[j, part], rows_send.at[j, q], rows_recv.at[j, q], (sec, dp, cls_peer(j))
        )

    def piece_copy(k):
        return remote(dp_out.at[k], dp_in.at[k], piece_send.at[k], piece_recv.at[k], (sec, dp_peer(k), cls))

    order = list(range(CHUNKS))[::-1]
    for q in order:
        for j in range(1, n_cls):
            for k in range(q * per_chunk, (q + 1) * per_chunk):
                cls_out[j, k] = gradient(k, cls_peer(j)).astype(jnp.bfloat16)
            rows_copy(j, q).start()
    for k in range(n_dp):
        kept[k] = gradient(k, cls)
    for q in order:
        for j in range(1, n_cls):
            rows_copy(j, q).wait_recv()
        for k in range(q * per_chunk, (q + 1) * per_chunk):
            value = kept[k]
            for j in range(1, n_cls):
                value = value + cls_in[j, k].astype(jnp.float32)
            if k == 0:
                kept[0] = value
            else:
                dp_out[k] = value.astype(jnp.bfloat16)
                piece_copy(k).start()

    rows = gathered[shard // n_group, lax.rem(shard, n_group)].astype(jnp.float32)
    norm = jnp.sqrt(jnp.sum(rows * rows, axis=1, keepdims=True) + EPSILON)
    inverse_norm = 1.0 / norm
    unit_rows = rows * inverse_norm
    unit_grad = kept[0]
    for k in list(range(1, n_dp))[::-1]:
        piece_copy(k).wait_recv()
        unit_grad = unit_grad + dp_in[k].astype(jnp.float32)
    along = jnp.sum(unit_rows * unit_grad, axis=1, keepdims=True)
    grad_ref[...] = (unit_grad - unit_rows * along) * inverse_norm

    for k in range(1, n_dp):
        block_copy(k).wait_send()
        label_copy(k).wait_send()
        sec_copy(k, sec).wait_send()
        all_copy(k).wait_send()
        piece_copy(k).wait_send()
        for j in range(1, n_cls):
            cls_copy(k, j).wait_send()
    for j in range(1, n_group):
        group_copy(j).wait_send()
    for copy in half_copies:
        copy.wait_send()
    for j in range(1, n_cls):
        for q in range(CHUNKS):
            rows_copy(j, q).wait_send()


def on_device(n_dp, n_cls, embeddings, centers, sample_ids, labels):
    block_rows, width = embeddings.shape
    n_pieces = 2 * n_cls
    rh = block_rows // n_pieces
    k_total = sample_ids.shape[1]
    rows = block_rows * n_dp
    half_pieces = n_dp * n_cls
    f32, bf16 = jnp.float32, jnp.bfloat16
    dma = pltpu.SemaphoreType.DMA
    vmem = pl.BlockSpec(memory_space=pltpu.VMEM)
    grad, loss = pl.pallas_call(
        functools.partial(kernel, n_dp, n_cls),
        out_shape=(
            jax.ShapeDtypeStruct((rh, width), f32),
            jax.ShapeDtypeStruct((1, block_rows), f32),
        ),
        in_specs=[vmem, pl.BlockSpec(memory_space=pl.ANY), vmem, vmem],
        out_specs=(vmem, vmem),
        scratch_shapes=[
            pltpu.VMEM(centers.shape, bf16),
            pltpu.VMEM((n_dp, n_pieces, rh, width), bf16),
            pltpu.VMEM((n_dp, 1, block_rows), jnp.int32),
            pltpu.VMEM((k_total, LANES), f32),
            pltpu.VMEM((k_total, width), bf16),
            pltpu.VMEM((rows, k_total), bf16),
            pltpu.VMEM((rows, k_total), bf16),
            pltpu.VMEM((n_dp, 2, block_rows), f32),
            pltpu.VMEM((n_pieces, n_dp, 2, block_rows), f32),
            pltpu.VMEM((n_dp, n_dp, 2, block_rows), f32),
            pltpu.VMEM((2, half_pieces, rh, width), f32),
            pltpu.VMEM((2, half_pieces, rh, width), bf16),
            pltpu.VMEM((half_pieces, rh, width), f32),
            pltpu.VMEM((half_pieces, rh, width), bf16),
            pltpu.VMEM((half_pieces, rh, LANES), f32),
            pltpu.VMEM((n_cls, n_dp, rh, width), bf16),
            pltpu.VMEM((n_cls, n_dp, rh, width), bf16),
            pltpu.VMEM((n_dp, rh, width), f32),
            pltpu.VMEM((n_dp, rh, width), bf16),
            pltpu.VMEM((n_dp, rh, width), bf16),
            dma,
            dma((n_dp,)), dma((n_dp,)), dma((n_dp,)), dma((n_dp,)),
            dma((n_cls, n_dp)), dma((n_cls, n_dp)), dma((n_dp,)), dma((n_dp,)),
            dma((n_pieces,)), dma((n_pieces,)), dma((n_dp,)), dma((n_dp,)),
            dma((2,)), dma((2,)),
            dma((n_cls, CHUNKS)), dma((n_cls, CHUNKS)), dma((n_dp,)), dma((n_dp,)),
        ],
        compiler_params=pltpu.CompilerParams(
            collective_id=0, has_side_effects=True, vmem_limit_bytes=52 * 1024 * 1024
        ),
    )(embeddings.reshape(n_pieces, rh, width), centers, sample_ids, labels.reshape(1, block_rows))
    return grad, loss.reshape(block_rows)


def solution(mesh):
    n_dp, n_cls = mesh.shape["dp"], mesh.shape["cls"]
    return jax.shard_map(
        functools.partial(on_device, n_dp, n_cls),
        mesh=mesh,
        in_specs=(
            P("dp", None),
            P(("section", "dp", "cls"), None),
            P(("section", "dp", "cls"), None),
            P("dp"),
        ),
        out_specs=(P(("section", "dp", "cls"), None), P("dp")),
        check_vma=False,
    )
```

```python
import functools

import jax
import jax.numpy as jnp
from jax import lax
from jax.experimental import pallas as pl
from jax.experimental.pallas import tpu as pltpu
from jax.sharding import PartitionSpec as P

LOGIT_SCALE = 64.0
MARGIN = 0.35
EPSILON = 1e-06
LANES = 128
PICK_STEPS = 4
UNIT = 4
CHUNKS = 4
MESH = pl.DeviceIdType.MESH


def to_column(row):
    return jnp.transpose(jnp.broadcast_to(row, (LANES, LANES)))


def to_row(column):
    return jnp.transpose(jnp.broadcast_to(column, (LANES, LANES)))[:1, :]


def kernel(
    n_dp, n_cls,
    emb_hbm, centers_hbm, ids_hbm, labels_hbm,
    grad_ref, loss_ref,
    centers, gathered, labels, ids_ref, ids_column, unit_centers, weights, onehot,
    sums, group_sums, all_sums,
    unscaled, own, unscaled_in, own_in, inverse,
    cls_out, cls_in, kept, dp_out, dp_in,
    centers_sem, inputs_sem,
    dp_send, dp_recv, label_send, label_recv, cls_send, cls_recv, sec_send, sec_recv,
    group_send, group_recv, all_send, all_recv, half_send, half_recv,
    rows_send, rows_recv, piece_send, piece_recv,
):
    sec, dp, cls = lax.axis_index("section"), lax.axis_index("dp"), lax.axis_index("cls")
    n_group = 2 * n_cls
    group = sec * n_cls + cls
    shard = (sec * n_dp + dp) * n_cls + cls
    other = 1 - sec
    n_pieces, rh, width = emb_hbm.shape
    per_shard = centers_hbm.shape[0]
    k_total = ids_hbm.shape[1]
    half_pieces = n_dp * n_cls
    pieces_per_unit = UNIT * n_pieces
    rows_per_unit = UNIT * LANES

    def dp_peer(k):
        return lax.rem(dp + k, n_dp)

    def dp_source(k):
        return lax.rem(dp + n_dp - k, n_dp)

    def cls_peer(j):
        return lax.rem(cls + j, n_cls)

    def group_peer(j):
        g = lax.rem(group + j, n_group)
        return (g // n_cls, dp, lax.rem(g, n_cls))

    def remote(src, dst, send, recv, device):
        return pltpu.make_async_remote_copy(
            src_ref=src, dst_ref=dst, send_sem=send, recv_sem=recv,
            device_id=device, device_id_type=MESH,
        )

    load = pltpu.make_async_copy(centers_hbm, centers, centers_sem)
    inputs = [
        pltpu.make_async_copy(ids_hbm, ids_ref, inputs_sem.at[0]),
        pltpu.make_async_copy(emb_hbm, gathered.at[dp], inputs_sem.at[1]),
        pltpu.make_async_copy(labels_hbm, labels.at[dp], inputs_sem.at[2]),
    ]
    for copy in inputs:
        copy.start()
    load.start()

    barrier = pltpu.get_barrier_semaphore()
    for k in range(1, n_dp):
        pl.semaphore_signal(barrier, inc=1, device_id=(sec, dp_peer(k), cls), device_id_type=MESH)
    for j in range(1, n_group):
        pl.semaphore_signal(barrier, inc=1, device_id=group_peer(j), device_id_type=MESH)

    for copy in inputs:
        copy.wait()
    ids_float = ids_ref[...].astype(jnp.float32)
    for i in range(k_total // LANES):
        ids_column[i * LANES:(i + 1) * LANES, :] = to_column(ids_float[:, i * LANES:(i + 1) * LANES])

    pl.semaphore_wait(barrier, n_dp - 1 + n_group - 1)

    def block_copy(k):
        return remote(
            gathered.at[dp, group], gathered.at[dp, group], dp_send.at[k], dp_recv.at[k], (sec, dp_peer(k), cls)
        )

    def block_arrival(k):
        there = gathered.at[dp_source(k), group]
        return remote(there, there, dp_send.at[k], dp_recv.at[k], (sec, dp_peer(k), cls))

    def label_copy(k):
        return remote(labels.at[dp], labels.at[dp], label_send.at[k], label_recv.at[k], (sec, dp_peer(k), cls))

    def label_arrival(k):
        there = labels.at[dp_source(k)]
        return remote(there, there, label_send.at[k], label_recv.at[k], (sec, dp_peer(k), cls))

    def cls_copy(k, j):
        piece = gathered.at[dp_source(k), group]
        return remote(piece, piece, cls_send.at[j, k], cls_recv.at[j, k], (sec, dp, cls_peer(j)))

    def cls_arrival(k, j):
        piece = gathered.at[dp_source(k), sec * n_cls + lax.rem(cls + n_cls - j, n_cls)]
        return remote(piece, piece, cls_send.at[j, k], cls_recv.at[j, k], (sec, dp, cls_peer(j)))

    def sec_copy(k, owner):
        pieces = gathered.at[dp_source(k), pl.ds(owner * n_cls, n_cls)]
        return remote(pieces, pieces, sec_send.at[k], sec_recv.at[k], (other, dp, cls))

    for k in range(1, n_dp):
        block_copy(k).start()
    for k in range(1, n_dp):
        label_copy(k).start()

    def pass_to_cls(k):
        block_arrival(k).wait_recv()
        for j in range(1, n_cls):
            cls_copy(k, j).start()

    def pass_to_sec(k):
        for j in range(1, n_cls):
            cls_arrival(k, j).wait_recv()
        sec_copy(k, sec).start()

    load.wait()
    step_rows = k_total // PICK_STEPS
    per_step = n_dp // PICK_STEPS
    lag = per_step

    def pick(t, carry):
        for i in range(per_step):
            k = t * per_step + i

            @pl.when(k >= 1)
            def _():
                pass_to_cls(k)

            @pl.when(k - lag >= 1)
            def _():
                pass_to_sec(k - lag)

        start = pl.multiple_of(t * step_rows, step_rows)
        wanted = ids_column[pl.ds(start, step_rows), :]
        lane = lax.broadcasted_iota(jnp.int32, (step_rows, LANES), 1).astype(jnp.float32)
        pieces = []
        for i in range(per_shard // LANES):
            hit = wanted == lane + jnp.float32(i * LANES)
            pieces.append(jnp.where(hit, jnp.float32(1.0), jnp.float32(0.0)).astype(jnp.bfloat16))
        chosen = jnp.dot(jnp.concatenate(pieces, axis=1), centers[...], preferred_element_type=jnp.float32)
        norm = jnp.sqrt(jnp.sum(chosen * chosen, axis=1, keepdims=True) + EPSILON)
        unit_centers[pl.ds(start, step_rows), :] = (chosen * (1.0 / norm)).astype(jnp.bfloat16)
        return carry

    lax.fori_loop(0, PICK_STEPS, pick, 0)
    for k in range(n_dp - lag, n_dp):
        pass_to_sec(k)
    for k in range(1, n_dp):
        label_arrival(k).wait_recv()
    for k in range(1, n_dp):
        sec_copy(k, other).wait_recv()

    def score(u, carry):
        rows = gathered[pl.ds(UNIT * u, UNIT)].astype(jnp.float32).reshape(rows_per_unit, width)
        norm = jnp.sqrt(jnp.sum(rows * rows, axis=1, keepdims=True) + EPSILON)
        unit_rows = (rows * (1.0 / norm)).astype(jnp.bfloat16)
        local = []
        for i in range(UNIT):
            local.append(to_column((labels[UNIT * u + i] - shard * per_shard).astype(jnp.float32)))
        local = jnp.concatenate(local, axis=0)
        cosine = lax.dot_general(
            unit_rows, unit_centers[...], (((1,), (1,)), ((), ())), preferred_element_type=jnp.float32
        )
        start = pl.multiple_of(u * rows_per_unit, rows_per_unit)
        total = jnp.zeros((rows_per_unit, LANES), jnp.float32)
        target = jnp.zeros((rows_per_unit, LANES), jnp.float32)
        for i in range(k_total // LANES):
            columns = slice(i * LANES, (i + 1) * LANES)
            matches = local == ids_ref[:, columns].astype(jnp.float32)
            logits = LOGIT_SCALE * cosine[:, columns]
            logits = jnp.where(matches, logits - LOGIT_SCALE * MARGIN, logits)
            exponent = jnp.exp(logits)
            total = total + exponent
            target = target + jnp.where(matches, logits, jnp.float32(0.0))
            weights[pl.ds(start, rows_per_unit), columns] = exponent.astype(jnp.bfloat16)
            onehot[pl.ds(start, rows_per_unit), columns] = jnp.where(
                matches, jnp.float32(1.0), jnp.float32(0.0)
            ).astype(jnp.bfloat16)
        total = jnp.sum(total, axis=1, keepdims=True)
        target = jnp.sum(target, axis=1, keepdims=True)
        for i in range(UNIT):
            part = slice(i * LANES, (i + 1) * LANES)
            sums[UNIT * u + i] = jnp.concatenate([to_row(total[part]), to_row(target[part])], axis=0)
        return carry

    lax.fori_loop(0, n_dp // UNIT, score, 0)

    group_sums[group] = sums[...]

    def group_copy(j):
        return remote(sums, group_sums.at[group], group_send.at[j], group_recv.at[j], group_peer(j))

    def group_arrival(j):
        there = group_sums.at[lax.rem(group + n_group - j, n_group)]
        return remote(there, there, group_send.at[j], group_recv.at[j], group_peer(j))

    def all_copy(k):
        return remote(
            all_sums.at[dp], all_sums.at[dp], all_send.at[k], all_recv.at[k], (sec, dp_peer(k), cls)
        )

    def all_arrival(k):
        there = all_sums.at[dp_source(k)]
        return remote(there, there, all_send.at[k], all_recv.at[k], (sec, dp_peer(k), cls))

    for j in range(1, n_group):
        group_copy(j).start()

    units_per_half = n_dp // (2 * UNIT)

    def weigh_half(half):
        def weigh(i, carry):
            u = half * units_per_half + i
            start = pl.multiple_of(u * rows_per_unit, rows_per_unit)
            dst = pl.ds(i * pieces_per_unit, pieces_per_unit)
            shape = (pieces_per_unit, rh, width)
            unscaled[half, dst] = jnp.dot(
                weights[pl.ds(start, rows_per_unit), :], unit_centers[...], preferred_element_type=jnp.float32
            ).reshape(shape)
            own[half, dst] = jnp.dot(
                onehot[pl.ds(start, rows_per_unit), :], unit_centers[...], preferred_element_type=jnp.float32
            ).reshape(shape).astype(jnp.bfloat16)
            return carry

        lax.fori_loop(0, units_per_half, weigh, 0)

    weigh_half(other)
    half_copies = [
        remote(unscaled.at[other], unscaled_in, half_send.at[0], half_recv.at[0], (other, dp, cls)),
        remote(own.at[other], own_in, half_send.at[1], half_recv.at[1], (other, dp, cls)),
    ]
    for copy in half_copies:
        copy.start()

    for j in range(1, n_group):
        group_arrival(j).wait_recv()
    group_total = group_sums[0]
    for j in range(1, n_group):
        group_total = group_total + group_sums[j]
    all_sums[dp] = group_total
    for k in range(1, n_dp):
        all_copy(k).start()

    weigh_half(sec)

    for k in range(1, n_dp):
        all_arrival(k).wait_recv()
    sums_all = all_sums[0]
    for k in range(1, n_dp):
        sums_all = sums_all + all_sums[k]
    group_sums[group] = sums_all
    mine = group_sums[group, dp]
    loss_ref[...] = jnp.log(mine[:1, :]) - mine[1:, :]
    for b in range(n_dp // 2):
        block = group_sums[group, sec * (n_dp // 2) + b]
        inverse[b * n_pieces:(b + 1) * n_pieces] = to_column(LOGIT_SCALE / block[:1, :]).reshape(
            n_pieces, rh, LANES
        )
    for copy in half_copies:
        copy.wait_recv()

    def gradient(k, column):
        p = dp_peer(k) * n_cls + column
        scale = jnp.concatenate([inverse[p]] * (width // LANES), axis=1)
        centers_here = own[sec, p].astype(jnp.float32) + own_in[p].astype(jnp.float32)
        return (unscaled[sec, p] + unscaled_in[p]) * scale - LOGIT_SCALE * centers_here

    per_chunk = n_dp // CHUNKS

    def rows_copy(j, q):
        part = pl.ds(q * per_chunk, per_chunk)
        return remote(
            cls_out.at[j, part], cls_in.at[j, part], rows_send.at[j, q], rows_recv.at[j, q], (sec, dp, cls_peer(j))
        )

    def piece_copy(k):
        return remote(dp_out.at[k], dp_in.at[k], piece_send.at[k], piece_recv.at[k], (sec, dp_peer(k), cls))

    order = list(range(CHUNKS))[::-1]
    for q in order:
        for j in range(1, n_cls):
            for k in range(q * per_chunk, (q + 1) * per_chunk):
                cls_out[j, k] = gradient(k, cls_peer(j)).astype(jnp.bfloat16)
            rows_copy(j, q).start()
    for k in range(n_dp):
        kept[k] = gradient(k, cls)
    for q in order:
        for j in range(1, n_cls):
            rows_copy(j, q).wait_recv()
        for k in range(q * per_chunk, (q + 1) * per_chunk):
            value = kept[k]
            for j in range(1, n_cls):
                value = value + cls_in[j, k].astype(jnp.float32)
            if k == 0:
                kept[0] = value
            else:
                dp_out[k] = value.astype(jnp.bfloat16)
                piece_copy(k).start()

    rows = gathered[shard // n_group, lax.rem(shard, n_group)].astype(jnp.float32)
    norm = jnp.sqrt(jnp.sum(rows * rows, axis=1, keepdims=True) + EPSILON)
    inverse_norm = 1.0 / norm
    unit_rows = rows * inverse_norm
    unit_grad = kept[0]
    for k in list(range(1, n_dp))[::-1]:
        piece_copy(k).wait_recv()
        unit_grad = unit_grad + dp_in[k].astype(jnp.float32)
    along = jnp.sum(unit_rows * unit_grad, axis=1, keepdims=True)
    grad_ref[...] = (unit_grad - unit_rows * along) * inverse_norm

    for k in range(1, n_dp):
        block_copy(k).wait_send()
        label_copy(k).wait_send()
        sec_copy(k, sec).wait_send()
        all_copy(k).wait_send()
        piece_copy(k).wait_send()
        for j in range(1, n_cls):
            cls_copy(k, j).wait_send()
    for j in range(1, n_group):
        group_copy(j).wait_send()
    for copy in half_copies:
        copy.wait_send()
    for j in range(1, n_cls):
        for q in range(CHUNKS):
            rows_copy(j, q).wait_send()


def on_device(n_dp, n_cls, embeddings, centers, sample_ids, labels):
    block_rows, width = embeddings.shape
    n_pieces = 2 * n_cls
    rh = block_rows // n_pieces
    k_total = sample_ids.shape[1]
    rows = block_rows * n_dp
    half_pieces = n_dp * n_cls
    f32, bf16 = jnp.float32, jnp.bfloat16
    dma = pltpu.SemaphoreType.DMA
    vmem = pl.BlockSpec(memory_space=pltpu.VMEM)
    grad, loss = pl.pallas_call(
        functools.partial(kernel, n_dp, n_cls),
        out_shape=(
            jax.ShapeDtypeStruct((rh, width), f32),
            jax.ShapeDtypeStruct((1, block_rows), f32),
        ),
        in_specs=[pl.BlockSpec(memory_space=pltpu.HBM)] * 4,
        out_specs=(vmem, vmem),
        scratch_shapes=[
            pltpu.VMEM(centers.shape, bf16),
            pltpu.VMEM((n_dp, n_pieces, rh, width), bf16),
            pltpu.VMEM((n_dp, 1, block_rows), jnp.int32),
            pltpu.VMEM((1, k_total), jnp.int32),
            pltpu.VMEM((k_total, LANES), f32),
            pltpu.VMEM((k_total, width), bf16),
            pltpu.VMEM((rows, k_total), bf16),
            pltpu.VMEM((rows, k_total), bf16),
            pltpu.VMEM((n_dp, 2, block_rows), f32),
            pltpu.VMEM((n_pieces, n_dp, 2, block_rows), f32),
            pltpu.VMEM((n_dp, n_dp, 2, block_rows), f32),
            pltpu.VMEM((2, half_pieces, rh, width), f32),
            pltpu.VMEM((2, half_pieces, rh, width), bf16),
            pltpu.VMEM((half_pieces, rh, width), f32),
            pltpu.VMEM((half_pieces, rh, width), bf16),
            pltpu.VMEM((half_pieces, rh, LANES), f32),
            pltpu.VMEM((n_cls, n_dp, rh, width), bf16),
            pltpu.VMEM((n_cls, n_dp, rh, width), bf16),
            pltpu.VMEM((n_dp, rh, width), f32),
            pltpu.VMEM((n_dp, rh, width), bf16),
            pltpu.VMEM((n_dp, rh, width), bf16),
            dma, dma((3,)),
            dma((n_dp,)), dma((n_dp,)), dma((n_dp,)), dma((n_dp,)),
            dma((n_cls, n_dp)), dma((n_cls, n_dp)), dma((n_dp,)), dma((n_dp,)),
            dma((n_pieces,)), dma((n_pieces,)), dma((n_dp,)), dma((n_dp,)),
            dma((2,)), dma((2,)),
            dma((n_cls, CHUNKS)), dma((n_cls, CHUNKS)), dma((n_dp,)), dma((n_dp,)),
        ],
        compiler_params=pltpu.CompilerParams(
            collective_id=0, has_side_effects=True, vmem_limit_bytes=52 * 1024 * 1024
        ),
    )(embeddings.reshape(n_pieces, rh, width), centers, sample_ids, labels.reshape(1, block_rows))
    return grad, loss.reshape(block_rows)


def solution(mesh):
    n_dp, n_cls = mesh.shape["dp"], mesh.shape["cls"]
    return jax.shard_map(
        functools.partial(on_device, n_dp, n_cls),
        mesh=mesh,
        in_specs=(
            P("dp", None),
            P(("section", "dp", "cls"), None),
            P(("section", "dp", "cls"), None),
            P("dp"),
        ),
        out_specs=(P(("section", "dp", "cls"), None), P("dp")),
        check_vma=False,
    )
```

```python
import functools

import jax
import jax.numpy as jnp
from jax import lax
from jax.experimental import pallas as pl
from jax.experimental.pallas import tpu as pltpu
from jax.sharding import PartitionSpec as P

LOGIT_SCALE = 64.0
MARGIN = 0.35
EPSILON = 1e-06
LANES = 128
PICK_STEPS = 4
UNIT = 4
CHUNKS = 4
MESH = pl.DeviceIdType.MESH


def to_column(row):
    return jnp.transpose(jnp.broadcast_to(row, (LANES, LANES)))


def to_row(column):
    return jnp.transpose(jnp.broadcast_to(column, (LANES, LANES)))[:1, :]


def kernel(
    n_dp, n_cls,
    emb_hbm, centers_hbm, ids_hbm, labels_hbm,
    grad_ref, loss_ref,
    centers, gathered, labels, ids_ref, ids_column, unit_centers, weights, onehot,
    sums, group_sums, all_sums,
    unscaled, own, unscaled_in, own_in, inverse,
    cls_out, cls_in, kept, dp_out, dp_in,
    centers_sem, inputs_sem,
    dp_send, dp_recv, label_send, label_recv, cls_send, cls_recv, sec_send, sec_recv,
    group_send, group_recv, all_send, all_recv, half_send, half_recv,
    rows_send, rows_recv, piece_send, piece_recv,
):
    sec, dp, cls = lax.axis_index("section"), lax.axis_index("dp"), lax.axis_index("cls")
    n_group = 2 * n_cls
    group = sec * n_cls + cls
    shard = (sec * n_dp + dp) * n_cls + cls
    other = 1 - sec
    n_pieces, rh, width = emb_hbm.shape
    per_shard = centers_hbm.shape[0]
    k_total = ids_hbm.shape[1]
    half_pieces = n_dp * n_cls
    pieces_per_unit = UNIT * n_pieces
    rows_per_unit = UNIT * LANES

    def dp_peer(k):
        return lax.rem(dp + k, n_dp)

    def dp_source(k):
        return lax.rem(dp + n_dp - k, n_dp)

    def cls_peer(j):
        return lax.rem(cls + j, n_cls)

    def group_peer(j):
        g = lax.rem(group + j, n_group)
        return (g // n_cls, dp, lax.rem(g, n_cls))

    def remote(src, dst, send, recv, device):
        return pltpu.make_async_remote_copy(
            src_ref=src, dst_ref=dst, send_sem=send, recv_sem=recv,
            device_id=device, device_id_type=MESH,
        )

    load = pltpu.make_async_copy(centers_hbm, centers, centers_sem)
    inputs = [
        pltpu.make_async_copy(ids_hbm, ids_ref, inputs_sem.at[0]),
        pltpu.make_async_copy(emb_hbm, gathered.at[dp], inputs_sem.at[1]),
        pltpu.make_async_copy(labels_hbm, labels.at[dp], inputs_sem.at[2]),
    ]
    for copy in inputs:
        copy.start()
    load.start()

    barrier = pltpu.get_barrier_semaphore()
    for k in range(1, n_dp):
        pl.semaphore_signal(barrier, inc=1, device_id=(sec, dp_peer(k), cls), device_id_type=MESH)
    for j in range(1, n_group):
        pl.semaphore_signal(barrier, inc=1, device_id=group_peer(j), device_id_type=MESH)

    for copy in inputs:
        copy.wait()
    ids_float = ids_ref[...].astype(jnp.float32)
    for i in range(k_total // LANES):
        ids_column[i * LANES:(i + 1) * LANES, :] = to_column(ids_float[:, i * LANES:(i + 1) * LANES])

    pl.semaphore_wait(barrier, n_dp - 1 + n_group - 1)

    def block_copy(k):
        return remote(
            gathered.at[dp, group], gathered.at[dp, group], dp_send.at[k], dp_recv.at[k], (sec, dp_peer(k), cls)
        )

    def block_arrival(k):
        there = gathered.at[dp_source(k), group]
        return remote(there, there, dp_send.at[k], dp_recv.at[k], (sec, dp_peer(k), cls))

    def label_copy(k):
        return remote(labels.at[dp], labels.at[dp], label_send.at[k], label_recv.at[k], (sec, dp_peer(k), cls))

    def label_arrival(k):
        there = labels.at[dp_source(k)]
        return remote(there, there, label_send.at[k], label_recv.at[k], (sec, dp_peer(k), cls))

    def cls_copy(k, j):
        piece = gathered.at[dp_source(k), group]
        return remote(piece, piece, cls_send.at[j, k], cls_recv.at[j, k], (sec, dp, cls_peer(j)))

    def cls_arrival(k, j):
        piece = gathered.at[dp_source(k), sec * n_cls + lax.rem(cls + n_cls - j, n_cls)]
        return remote(piece, piece, cls_send.at[j, k], cls_recv.at[j, k], (sec, dp, cls_peer(j)))

    def sec_copy(k, owner):
        pieces = gathered.at[dp_source(k), pl.ds(owner * n_cls, n_cls)]
        return remote(pieces, pieces, sec_send.at[k], sec_recv.at[k], (other, dp, cls))

    for k in range(1, n_dp):
        block_copy(k).start()
    for k in range(1, n_dp):
        label_copy(k).start()

    def pass_to_cls(k):
        block_arrival(k).wait_recv()
        for j in range(1, n_cls):
            cls_copy(k, j).start()

    def pass_to_sec(k):
        for j in range(1, n_cls):
            cls_arrival(k, j).wait_recv()
        sec_copy(k, sec).start()

    load.wait()
    step_rows = k_total // PICK_STEPS
    per_step = n_dp // PICK_STEPS

    def pick(t, carry):
        for i in range(per_step):
            k = t * per_step + i

            @pl.when(t >= 1)
            def _():
                pass_to_cls(k)

            @pl.when(t >= 2)
            def _():
                pass_to_sec(k - per_step)

        for k in range(1, per_step):
            @pl.when(t == 1)
            def _():
                pass_to_cls(k)

            @pl.when(t == 2)
            def _():
                pass_to_sec(k)

        start = pl.multiple_of(t * step_rows, step_rows)
        wanted = ids_column[pl.ds(start, step_rows), :]
        lane = lax.broadcasted_iota(jnp.int32, (step_rows, LANES), 1).astype(jnp.float32)
        pieces = []
        for i in range(per_shard // LANES):
            hit = wanted == lane + jnp.float32(i * LANES)
            pieces.append(jnp.where(hit, jnp.float32(1.0), jnp.float32(0.0)).astype(jnp.bfloat16))
        chosen = jnp.dot(jnp.concatenate(pieces, axis=1), centers[...], preferred_element_type=jnp.float32)
        norm = jnp.sqrt(jnp.sum(chosen * chosen, axis=1, keepdims=True) + EPSILON)
        unit_centers[pl.ds(start, step_rows), :] = (chosen * (1.0 / norm)).astype(jnp.bfloat16)
        return carry

    lax.fori_loop(0, PICK_STEPS, pick, 0)
    for k in range(n_dp - per_step, n_dp):
        pass_to_sec(k)
    for k in range(1, n_dp):
        label_arrival(k).wait_recv()

    def score(u, carry):
        for i in range(UNIT):
            k = UNIT * u + i

            @pl.when(k >= 1)
            def _():
                sec_copy(k, other).wait_recv()

        blocks = [dp_source(UNIT * u + i) for i in range(UNIT)]
        starts = [pl.multiple_of(b * LANES, LANES) for b in blocks]
        rows = [gathered[b].reshape(LANES, width) for b in blocks]
        rows = jnp.concatenate(rows, axis=0).astype(jnp.float32)
        norm = jnp.sqrt(jnp.sum(rows * rows, axis=1, keepdims=True) + EPSILON)
        unit_rows = (rows * (1.0 / norm)).astype(jnp.bfloat16)
        local = []
        for i in range(UNIT):
            local.append(to_column((labels[blocks[i]] - shard * per_shard).astype(jnp.float32)))
        local = jnp.concatenate(local, axis=0)
        cosine = lax.dot_general(
            unit_rows, unit_centers[...], (((1,), (1,)), ((), ())), preferred_element_type=jnp.float32
        )
        total = jnp.zeros((rows_per_unit, LANES), jnp.float32)
        target = jnp.zeros((rows_per_unit, LANES), jnp.float32)
        for i in range(k_total // LANES):
            columns = slice(i * LANES, (i + 1) * LANES)
            matches = local == ids_ref[:, columns].astype(jnp.float32)
            logits = LOGIT_SCALE * cosine[:, columns]
            logits = jnp.where(matches, logits - LOGIT_SCALE * MARGIN, logits)
            exponent = jnp.exp(logits)
            total = total + exponent
            target = target + jnp.where(matches, logits, jnp.float32(0.0))
            exponent = exponent.astype(jnp.bfloat16)
            hits = jnp.where(matches, jnp.float32(1.0), jnp.float32(0.0)).astype(jnp.bfloat16)
            for b in range(UNIT):
                weights[pl.ds(starts[b], LANES), columns] = exponent[b * LANES:(b + 1) * LANES]
                onehot[pl.ds(starts[b], LANES), columns] = hits[b * LANES:(b + 1) * LANES]
        total = jnp.sum(total, axis=1, keepdims=True)
        target = jnp.sum(target, axis=1, keepdims=True)
        for i in range(UNIT):
            part = slice(i * LANES, (i + 1) * LANES)
            sums[blocks[i]] = jnp.concatenate([to_row(total[part]), to_row(target[part])], axis=0)
        return carry

    lax.fori_loop(0, n_dp // UNIT, score, 0)

    group_sums[group] = sums[...]

    def group_copy(j):
        return remote(sums, group_sums.at[group], group_send.at[j], group_recv.at[j], group_peer(j))

    def group_arrival(j):
        there = group_sums.at[lax.rem(group + n_group - j, n_group)]
        return remote(there, there, group_send.at[j], group_recv.at[j], group_peer(j))

    def all_copy(k):
        return remote(
            all_sums.at[dp], all_sums.at[dp], all_send.at[k], all_recv.at[k], (sec, dp_peer(k), cls)
        )

    def all_arrival(k):
        there = all_sums.at[dp_source(k)]
        return remote(there, there, all_send.at[k], all_recv.at[k], (sec, dp_peer(k), cls))

    for j in range(1, n_group):
        group_copy(j).start()

    units_per_half = n_dp // (2 * UNIT)

    def weigh_half(half):
        def weigh(i, carry):
            u = half * units_per_half + i
            start = pl.multiple_of(u * rows_per_unit, rows_per_unit)
            dst = pl.ds(i * pieces_per_unit, pieces_per_unit)
            shape = (pieces_per_unit, rh, width)
            unscaled[half, dst] = jnp.dot(
                weights[pl.ds(start, rows_per_unit), :], unit_centers[...], preferred_element_type=jnp.float32
            ).reshape(shape)
            own[half, dst] = jnp.dot(
                onehot[pl.ds(start, rows_per_unit), :], unit_centers[...], preferred_element_type=jnp.float32
            ).reshape(shape).astype(jnp.bfloat16)
            return carry

        lax.fori_loop(0, units_per_half, weigh, 0)

    weigh_half(other)
    half_copies = [
        remote(unscaled.at[other], unscaled_in, half_send.at[0], half_recv.at[0], (other, dp, cls)),
        remote(own.at[other], own_in, half_send.at[1], half_recv.at[1], (other, dp, cls)),
    ]
    for copy in half_copies:
        copy.start()

    for j in range(1, n_group):
        group_arrival(j).wait_recv()
    group_total = group_sums[0]
    for j in range(1, n_group):
        group_total = group_total + group_sums[j]
    all_sums[dp] = group_total
    for k in range(1, n_dp):
        all_copy(k).start()

    weigh_half(sec)

    for k in range(1, n_dp):
        all_arrival(k).wait_recv()
    sums_all = all_sums[0]
    for k in range(1, n_dp):
        sums_all = sums_all + all_sums[k]
    group_sums[group] = sums_all
    mine = group_sums[group, dp]
    loss_ref[...] = jnp.log(mine[:1, :]) - mine[1:, :]
    for b in range(n_dp // 2):
        block = group_sums[group, sec * (n_dp // 2) + b]
        inverse[b * n_pieces:(b + 1) * n_pieces] = to_column(LOGIT_SCALE / block[:1, :]).reshape(
            n_pieces, rh, LANES
        )
    for copy in half_copies:
        copy.wait_recv()

    def gradient(k, column):
        p = dp_peer(k) * n_cls + column
        scale = jnp.concatenate([inverse[p]] * (width // LANES), axis=1)
        centers_here = own[sec, p].astype(jnp.float32) + own_in[p].astype(jnp.float32)
        return (unscaled[sec, p] + unscaled_in[p]) * scale - LOGIT_SCALE * centers_here

    per_chunk = n_dp // CHUNKS

    def rows_copy(j, q):
        part = pl.ds(q * per_chunk, per_chunk)
        return remote(
            cls_out.at[j, part], cls_in.at[j, part], rows_send.at[j, q], rows_recv.at[j, q], (sec, dp, cls_peer(j))
        )

    def piece_copy(k):
        return remote(dp_out.at[k], dp_in.at[k], piece_send.at[k], piece_recv.at[k], (sec, dp_peer(k), cls))

    order = list(range(CHUNKS))[::-1]
    for q in order:
        for j in range(1, n_cls):
            for k in range(q * per_chunk, (q + 1) * per_chunk):
                cls_out[j, k] = gradient(k, cls_peer(j)).astype(jnp.bfloat16)
            rows_copy(j, q).start()
    for k in range(n_dp):
        kept[k] = gradient(k, cls)
    for q in order:
        for j in range(1, n_cls):
            rows_copy(j, q).wait_recv()
        for k in range(q * per_chunk, (q + 1) * per_chunk):
            value = kept[k]
            for j in range(1, n_cls):
                value = value + cls_in[j, k].astype(jnp.float32)
            if k == 0:
                kept[0] = value
            else:
                dp_out[k] = value.astype(jnp.bfloat16)
                piece_copy(k).start()

    rows = gathered[shard // n_group, lax.rem(shard, n_group)].astype(jnp.float32)
    norm = jnp.sqrt(jnp.sum(rows * rows, axis=1, keepdims=True) + EPSILON)
    inverse_norm = 1.0 / norm
    unit_rows = rows * inverse_norm
    unit_grad = kept[0]
    for k in list(range(1, n_dp))[::-1]:
        piece_copy(k).wait_recv()
        unit_grad = unit_grad + dp_in[k].astype(jnp.float32)
    along = jnp.sum(unit_rows * unit_grad, axis=1, keepdims=True)
    grad_ref[...] = (unit_grad - unit_rows * along) * inverse_norm

    for k in range(1, n_dp):
        block_copy(k).wait_send()
        label_copy(k).wait_send()
        sec_copy(k, sec).wait_send()
        all_copy(k).wait_send()
        piece_copy(k).wait_send()
        for j in range(1, n_cls):
            cls_copy(k, j).wait_send()
    for j in range(1, n_group):
        group_copy(j).wait_send()
    for copy in half_copies:
        copy.wait_send()
    for j in range(1, n_cls):
        for q in range(CHUNKS):
            rows_copy(j, q).wait_send()


def on_device(n_dp, n_cls, embeddings, centers, sample_ids, labels):
    block_rows, width = embeddings.shape
    n_pieces = 2 * n_cls
    rh = block_rows // n_pieces
    k_total = sample_ids.shape[1]
    rows = block_rows * n_dp
    half_pieces = n_dp * n_cls
    f32, bf16 = jnp.float32, jnp.bfloat16
    dma = pltpu.SemaphoreType.DMA
    vmem = pl.BlockSpec(memory_space=pltpu.VMEM)
    grad, loss = pl.pallas_call(
        functools.partial(kernel, n_dp, n_cls),
        out_shape=(
            jax.ShapeDtypeStruct((rh, width), f32),
            jax.ShapeDtypeStruct((1, block_rows), f32),
        ),
        in_specs=[pl.BlockSpec(memory_space=pltpu.HBM)] * 4,
        out_specs=(vmem, vmem),
        scratch_shapes=[
            pltpu.VMEM(centers.shape, bf16),
            pltpu.VMEM((n_dp, n_pieces, rh, width), bf16),
            pltpu.VMEM((n_dp, 1, block_rows), jnp.int32),
            pltpu.VMEM((1, k_total), jnp.int32),
            pltpu.VMEM((k_total, LANES), f32),
            pltpu.VMEM((k_total, width), bf16),
            pltpu.VMEM((rows, k_total), bf16),
            pltpu.VMEM((rows, k_total), bf16),
            pltpu.VMEM((n_dp, 2, block_rows), f32),
            pltpu.VMEM((n_pieces, n_dp, 2, block_rows), f32),
            pltpu.VMEM((n_dp, n_dp, 2, block_rows), f32),
            pltpu.VMEM((2, half_pieces, rh, width), f32),
            pltpu.VMEM((2, half_pieces, rh, width), bf16),
            pltpu.VMEM((half_pieces, rh, width), f32),
            pltpu.VMEM((half_pieces, rh, width), bf16),
            pltpu.VMEM((half_pieces, rh, LANES), f32),
            pltpu.VMEM((n_cls, n_dp, rh, width), bf16),
            pltpu.VMEM((n_cls, n_dp, rh, width), bf16),
            pltpu.VMEM((n_dp, rh, width), f32),
            pltpu.VMEM((n_dp, rh, width), bf16),
            pltpu.VMEM((n_dp, rh, width), bf16),
            dma, dma((3,)),
            dma((n_dp,)), dma((n_dp,)), dma((n_dp,)), dma((n_dp,)),
            dma((n_cls, n_dp)), dma((n_cls, n_dp)), dma((n_dp,)), dma((n_dp,)),
            dma((n_pieces,)), dma((n_pieces,)), dma((n_dp,)), dma((n_dp,)),
            dma((2,)), dma((2,)),
            dma((n_cls, CHUNKS)), dma((n_cls, CHUNKS)), dma((n_dp,)), dma((n_dp,)),
        ],
        compiler_params=pltpu.CompilerParams(
            collective_id=0, has_side_effects=True, vmem_limit_bytes=52 * 1024 * 1024
        ),
    )(embeddings.reshape(n_pieces, rh, width), centers, sample_ids, labels.reshape(1, block_rows))
    return grad, loss.reshape(block_rows)


def solution(mesh):
    n_dp, n_cls = mesh.shape["dp"], mesh.shape["cls"]
    return jax.shard_map(
        functools.partial(on_device, n_dp, n_cls),
        mesh=mesh,
        in_specs=(
            P("dp", None),
            P(("section", "dp", "cls"), None),
            P(("section", "dp", "cls"), None),
            P("dp"),
        ),
        out_specs=(P(("section", "dp", "cls"), None), P("dp")),
        check_vma=False,
    )
```
